32 devices in a mesh: dp: 8 (over y, x, core), tensor: 4 (over z).
Axes of the slice: x: 2, y: 2, z: 4, core: 2. Of those that a mesh axis runs over, the one named last changes fastest.
Arguments:
- tokens: bfloat16 [8192, 8192], P('dp', 'tensor'), may hold values from -6 to 6
- packing: int32 [8, 6], replicated, may hold values from 0 to 63, as said below
- tail_tokens: int32 [8], replicated, may hold values from 1 to 128
- mix_ratio: int32 [2], replicated, may hold values from 1 to 32, as said below
- policy_gate: bfloat16 [8192, 14336], P(('dp', 'tensor')), may hold values from -6 to 6
- policy_up: bfloat16 [8192, 14336], P(('dp', 'tensor')), may hold values from -6 to 6
- reference_gate: bfloat16 [8192, 14336], P('dp', 'tensor'), may hold values from -6 to 6
- reference_up: bfloat16 [8192, 14336], P('dp', 'tensor'), may hold values from -6 to 6
Outputs:
- new_gate: bfloat16 [8192, 14336], P('dp', 'tensor')
- new_up: bfloat16 [8192, 14336], P('dp', 'tensor')
- hidden: bfloat16 [6144, 14336], P('dp', 'tensor')
The draws below stay inside these ranges and needn't reach their ends.
Inputs may be any that keep to these rules, and one draw needn't show every extreme that they name: `packing`: each entry is g * 8 + b for a data group g and block b; the blocks named for group g are exactly its blocks 0 to count - 1, each once; a reference group takes at most one block from any data group; one data group has all 8 of its blocks named. mix_ratio[1] is 32 and mix_ratio[0] lies between 1 and 31.
All inputs are finite; a program needn't handle non-finite values.
Results may differ from the reference program's by a relative error of at most 0.02.
Values may be sent and summed in bfloat16 or wider, within the bound.
A program may use at most 256 MiB of HBM per device.

```python
import math
import jax
import jax.numpy as jnp
from jax import lax

D = 8192
FFW = 14336
BLOCK = 128
GB = 6
SB = 8
N_DP = 8


def draw_packing(key, part):
    first_key = jax.random.fold_in(key, 11)
    second_key = jax.random.fold_in(key, 12)
    third_key = jax.random.fold_in(key, 13)
    order = jax.random.permutation(first_key, N_DP).astype(jnp.int32)
    others = order[1:]
    offset = jax.random.randint(second_key, (), 0, N_DP - 1)
    dest_ids = jnp.arange(N_DP, dtype=jnp.int32)[:, None]
    slot_ids = jnp.arange(GB, dtype=jnp.int32)[None, :]
    spread_index = (dest_ids * (GB - 1) + slot_ids - 1 + offset) % (N_DP - 1)
    sources = jnp.where(slot_ids == 0, order[0], others[spread_index])
    flat_sources = sources.reshape(-1)
    one_hot = (flat_sources[:, None] == jnp.arange(N_DP, dtype=jnp.int32)[None, :]).astype(jnp.int32)
    earlier = jnp.cumsum(one_hot, axis=0) - one_hot
    block_ids = jnp.sum(earlier * one_hot, axis=1)
    entries = (flat_sources * SB + block_ids).reshape(N_DP, GB)
    row_keys = jax.random.split(third_key, N_DP)
    shuffles = jax.vmap(lambda row_key: jax.random.permutation(row_key, GB))(row_keys)
    return jnp.take_along_axis(entries, shuffles, axis=1).astype(jnp.int32)


def draw_mix_ratio(key, part):
    numer_key = jax.random.fold_in(key, 22)
    denominator = jnp.full((), 32, jnp.int32)
    numerator = jax.random.randint(numer_key, (), 1, 32)
    return jnp.stack([numerator, denominator]).astype(jnp.int32)


def touch_ends(array, own_key, low, high):
    shape = array.shape
    place = [jax.random.randint(jax.random.fold_in(own_key, axis), (), 0, shape[axis]) for axis in range(len(shape))]
    array = array.at[tuple(place)].set(low)
    longest = shape.index(max(shape))
    place[longest] = (place[longest] + 1) % shape[longest]
    return array.at[tuple(place)].set(high)


def level_of(rng, dims, cuts, least, largest):
    factor_of, own = 1.0, jax.random.fold_in(rng, 6)
    for position, blocks in cuts:
        heights = jnp.exp(jax.random.uniform(jax.random.fold_in(own, position), (blocks,), jnp.float32, least / len(cuts), largest / len(cuts)))
        factor_of = factor_of * jnp.repeat(heights, dims[position] // blocks).reshape([-1 if axis == position else 1 for axis in range(len(dims))])
    return factor_of


def scatter_about(key, extent, deviation, limit, cuts=(), held_as=jnp.bfloat16):
    values = jax.random.normal(key, extent, jnp.float32) * deviation
    if len(cuts) > 0:
        values = level_of(key, extent, cuts, -0.22, 0.18) * values
    return jnp.clip(values, min=-limit, max=limit).astype(held_as)


def setup_inputs(seed: int = 0) -> dict:
    splits = jax.random.split(jax.random.key(seed), 9)
    return {
        "tokens": scatter_about(splits[0], (N_DP * SB * BLOCK, D), 1.0, 6.0, ((0, 8), (1, 4))),
        "packing": draw_packing(jax.random.fold_in(splits[8], 71), 0),
        "tail_tokens": touch_ends(jax.random.randint(splits[2], (N_DP,), 1, BLOCK + 1), jax.random.fold_in(splits[2], 1), 1, BLOCK).astype(jnp.int32),
        "mix_ratio": draw_mix_ratio(jax.random.fold_in(splits[8], 71), 0),
        "policy_gate": scatter_about(splits[4], (D, FFW), 1.0, 6.0, ((0, 32),)),
        "policy_up": scatter_about(splits[5], (D, FFW), 1.0, 6.0, ((0, 32),)),
        "reference_gate": scatter_about(splits[6], (D, FFW), 1.0, 6.0, ((0, 8), (1, 4))),
        "reference_up": scatter_about(splits[7], (D, FFW), 1.0, 6.0, ((0, 8), (1, 4))),
    }


def blend_into(policy_part, old_part, weight_ratio):
    mixed = weight_ratio * policy_part.astype(jnp.float32) + (1.0 - weight_ratio) * old_part.astype(jnp.float32)
    return mixed.astype(jnp.bfloat16)

def reference(tokens, packing, tail_tokens, mix_ratio, policy_gate, policy_up, reference_gate, reference_up):
    weight_ratio = mix_ratio[0].astype(jnp.float32) / mix_ratio[1].astype(jnp.float32)
    new_gate = blend_into(policy_gate, reference_gate, weight_ratio)
    new_up = blend_into(policy_up, reference_up, weight_ratio)
    source = packing // SB
    group_ids = jnp.arange(N_DP, dtype=jnp.int32)
    counts = lax.optimization_barrier(jnp.sum((source.reshape(-1)[:, None] == group_ids[None, :]).astype(jnp.int32), axis=0))
    row_limit = (counts - 1) * BLOCK + tail_tokens
    grouped = tokens.reshape(N_DP, SB * BLOCK, D)
    keep_mask = jnp.arange(SB * BLOCK, dtype=jnp.int32)[None, :] < row_limit[:, None]
    masked_rows = jnp.where(keep_mask[:, :, None], grouped, jnp.zeros((), jnp.bfloat16))
    blocks = masked_rows.reshape(N_DP * SB, BLOCK, D)
    packed = jnp.take(blocks, packing.reshape(-1).astype(jnp.int32), axis=0).reshape(N_DP * GB * BLOCK, D)
    row_width = D // N_DP
    row_total = N_DP * GB * BLOCK
    packed_blocks = packed.reshape(row_total, N_DP, row_width).transpose(1, 0, 2)
    gate_blocks = new_gate.reshape(N_DP, row_width, FFW)
    up_blocks = new_up.reshape(N_DP, row_width, FFW)

    def add_block(carry, items):
        columns, gate_rows, up_rows = items
        gate_part = jnp.dot(columns, gate_rows, preferred_element_type=jnp.float32).astype(jnp.bfloat16)
        up_part = jnp.dot(columns, up_rows, preferred_element_type=jnp.float32).astype(jnp.bfloat16)
        return ((carry[0] + gate_part.astype(jnp.float32), carry[1] + up_part.astype(jnp.float32)), None)
    start = (jnp.zeros((row_total, FFW), jnp.float32), jnp.zeros((row_total, FFW), jnp.float32))
    totals, unused = lax.scan(add_block, start, (packed_blocks, gate_blocks, up_blocks))
    inv_width = 1.0 / math.sqrt(D)
    gate_sum = totals[0] * inv_width
    up_sum = totals[1] * inv_width
    hidden = (jax.nn.silu(gate_sum) * up_sum).astype(jnp.bfloat16)
    return (new_gate, new_up, hidden)
```

```python
import math

import jax
import jax.numpy as jnp
from jax import lax
from jax.sharding import PartitionSpec as P

BLOCK = 128
UNITS = 28
CHUNKS = (4, 8, 8, 8)


def blend_into(policy_part, old_part, weight_ratio):
    mixed = weight_ratio * policy_part.astype(jnp.float32) + (1.0 - weight_ratio) * old_part.astype(
        jnp.float32
    )
    return mixed.astype(jnp.bfloat16)


def shift_perm(count, shift):
    return [(i, (i + shift) % count) for i in range(count)]


def body(
    tokens, packing, tail_tokens, mix_ratio, policy_gate, policy_up, reference_gate, reference_up
):
    weight_ratio = mix_ratio[0].astype(jnp.float32) / mix_ratio[1].astype(jnp.float32)
    planes = lax.axis_size("tensor")
    my_plane = lax.axis_index("tensor")
    rows = policy_gate.shape[0]
    width = reference_gate.shape[1]

    pieces = []
    edge = 0
    for units in CHUNKS:
        cols = width * units // UNITS
        chunk = []
        for policy in (policy_gate, policy_up):
            got = []
            for shift in range(planes):
                target = lax.rem(my_plane + shift, planes)
                piece = lax.dynamic_slice(policy, (0, target * width + edge), (rows, cols))
                if shift:
                    piece = lax.ppermute(piece, "tensor", shift_perm(planes, shift))
                got.append(piece)
            chunk.append(got)
        pieces.append((edge, cols, chunk))
        edge += cols

    groups = packing.shape[0]
    slot_count = packing.shape[1]
    per_group = tokens.shape[0]
    feats = tokens.shape[1]
    my_group = lax.axis_index("dp")
    source = packing // groups
    group_ids = jnp.arange(groups, dtype=jnp.int32)
    counts = jnp.sum((source.reshape(-1)[:, None] == group_ids[None, :]).astype(jnp.int32), axis=0)
    row_limit = (counts[my_group] - 1) * BLOCK + tail_tokens[my_group]
    blocks = tokens.reshape(per_group // BLOCK, BLOCK, feats)
    from_here = source == my_group
    chosen = jnp.sum(jnp.where(from_here, packing % groups, 0), axis=1)
    block_row = jnp.arange(BLOCK, dtype=jnp.int32)
    keep = (chosen[:, None] * BLOCK + block_row[None, :]) < row_limit
    outgoing = jnp.where(keep[:, :, None], jnp.take(blocks, chosen, axis=0), jnp.zeros((), jnp.bfloat16))
    arrived = lax.all_to_all(outgoing, "dp", split_axis=0, concat_axis=0, tiled=True)
    packed = jnp.take(arrived, source[my_group], axis=0).reshape(slot_count * BLOCK, feats)
    full_rows = jnp.zeros((slot_count * BLOCK, feats * planes), jnp.bfloat16)
    for shift in range(planes):
        origin = lax.rem(my_plane + planes - shift, planes)
        part = packed if shift == 0 else lax.ppermute(packed, "tensor", shift_perm(planes, shift))
        full_rows = lax.dynamic_update_slice(full_rows, part, (0, origin * feats))

    inv_width = 1.0 / math.sqrt(full_rows.shape[1])
    new_parts = ([], [])
    hidden_parts = []
    for edge, cols, chunk in pieces:
        sums = []
        for which, (old, got) in enumerate(zip((reference_gate, reference_up), chunk)):
            new = jnp.zeros((rows * planes, cols), jnp.bfloat16)
            for shift in range(planes):
                origin = lax.rem(my_plane + planes - shift, planes)
                old_part = lax.dynamic_slice(old, (origin * rows, edge), (rows, cols))
                new = lax.dynamic_update_slice(
                    new, blend_into(got[shift], old_part, weight_ratio), (origin * rows, 0)
                )
            new_parts[which].append(new)
            gathered = lax.all_gather(new, "dp", axis=0, tiled=True)
            sums.append(jnp.dot(full_rows, gathered, preferred_element_type=jnp.float32) * inv_width)
        hidden_parts.append((jax.nn.silu(sums[0]) * sums[1]).astype(jnp.bfloat16))
    return (
        jnp.concatenate(new_parts[0], axis=1),
        jnp.concatenate(new_parts[1], axis=1),
        jnp.concatenate(hidden_parts, axis=1),
    )


def solution(mesh):
    in_specs = (
        P("dp", "tensor"),
        P(),
        P(),
        P(),
        P(("dp", "tensor"), None),
        P(("dp", "tensor"), None),
        P("dp", "tensor"),
        P("dp", "tensor"),
    )
    out_specs = (P("dp", "tensor"), P("dp", "tensor"), P("dp", "tensor"))
    return jax.shard_map(body, mesh=mesh, in_specs=in_specs, out_specs=out_specs, check_vma=False)
```
